32 devices in a mesh: gx: 4 (over z), gy: 2 (over y), gz: 4 (over x, core).
Axes of the slice: x: 2, y: 2, z: 4, core: 2. Of those that a mesh axis runs over, the one named last changes fastest.
Arguments:
- adjoint_fields: float32 [6, 1, 16, 16, 512], P(None, None, 'gx', 'gy', 'gz'), may hold values from -6 to 6
- forward_fields: bfloat16 [2, 3, 1, 16, 16, 512], P(None, None, None, 'gx', 'gy', 'gz'), may hold values from -6 to 6
- rock_unit: int32 [16, 16, 512], P('gx', 'gy', 'gz'), may hold values from 0 to 31
- unit_conductivity: int32 [32], replicated, may hold values from 50 to 2000
- receiver_cells: int32 [256], replicated, may hold values from 0 to 131071
- residuals: float32 [2, 1, 256], replicated, may hold values from -6 to 6
- model_vectors: float32 [16, 4, 16, 512], P('gx', None, 'gy', 'gz'), may hold values from -6 to 6
Outputs:
- adjoint_state: float32 [6, 1, 16, 16, 512], P(None, None, 'gx', 'gy', 'gz')
- normal_product: float32 [16, 4, 16, 512], P('gx', None, 'gy', 'gz')
The draws below stay inside these ranges and needn't reach their ends.
Inputs may be any that keep to these rules, and one draw needn't show every extreme that they name: `rock_unit`: each entry is a rock unit number. `receiver_cells`: a receiver's linear cell index; two receivers may share a cell.
All inputs are finite; a program needn't handle non-finite values.
Results may differ from the reference program's by a relative error of at most 0.00075.
Values sent between devices are 32-bit elements; how exact they have to be, the bound alone decides.
A program may use at most 64 MiB of HBM per device.

```python
import jax
import jax.numpy as jnp
from jax import lax

S = 1
STEPS = 2
R = 256
U = 32
NV = 4
NX = 16
NY = 16
NZ = 512


def touch_ends(values, rng, low, top_value):
    place = [jax.random.randint(jax.random.fold_in(rng, axis), (), 0, length) for axis, length in enumerate(values.shape)]
    longest = values.shape.index(max(values.shape))
    beside = place[:longest] + [(place[longest] + 1) % values.shape[longest]] + place[longest + 1:]
    return values.at[tuple(place)].set(low).at[tuple(beside)].set(top_value)


def steps_of(own_key, dims, cuts, smallest, top_value):
    level = 1.0
    for position, parts in cuts:
        draws = jax.random.uniform(jax.random.fold_in(jax.random.fold_in(own_key, 6), position), (parts,), jnp.float32, smallest / len(cuts), top_value / len(cuts))
        level = level * jnp.repeat(jnp.exp(draws), dims[position] // parts).reshape((-1,) + (1,) * (len(dims) - 1 - position))
    return level


def bell_draw(key, shape, deviation, limit, split=(), kind=jnp.bfloat16):
    array = jax.random.normal(key, shape, jnp.float32) * deviation
    if len(split) > 0:
        array = steps_of(key, shape, split, -0.22, 0.18) * array
    return jnp.clip(array, min=-limit, max=limit).astype(kind)


def setup_inputs(seed: int = 0) -> dict:
    streams_of = jax.random.split(jax.random.key(seed), 8)
    adjoint_fields = bell_draw(streams_of[0], (6, S, NX, NY, NZ), 1.0, 6.0, ((2, 4), (3, 2), (4, 4)), jnp.float32)
    forward_fields = bell_draw(streams_of[1], (STEPS, 3, S, NX, NY, NZ), 1.0, 6.0, ((3, 4), (4, 2), (5, 4)))
    rock_unit = touch_ends(jax.random.randint(streams_of[2], (NX, NY, NZ), 0, U), jax.random.fold_in(streams_of[2], 1), 0, U - 1).astype(jnp.int32)
    unit_conductivity = touch_ends(jax.random.randint(streams_of[3], (U,), 50, 2001), jax.random.fold_in(streams_of[3], 1), 50, 2000).astype(jnp.int32)
    receiver_cells = touch_ends(jax.random.randint(streams_of[4], (R,), 0, NX * NY * NZ), jax.random.fold_in(streams_of[4], 1), 0, (NX * NY * NZ) - 1).astype(jnp.int32)
    residuals = bell_draw(streams_of[5], (STEPS, S, R), 1.0, 6.0, (), jnp.float32)
    model_vectors = bell_draw(streams_of[6], (NX, NV, NY, NZ), 1.0, 6.0, ((0, 4), (2, 2), (3, 4)), jnp.float32)
    return {"adjoint_fields": adjoint_fields, "forward_fields": forward_fields, "rock_unit": rock_unit, "unit_conductivity": unit_conductivity, "receiver_cells": receiver_cells, "residuals": residuals, "model_vectors": model_vectors}


LOSS_FACTOR = 0.5
COURANT = 0.5

def advance(state, forward_now, conductivity, keep_rate, drive_rate, inject):
    electric = state[0:3]
    magnetic = state[3:6]
    forward_f = forward_now.astype(jnp.float32)
    panel = conductivity * (forward_f[0] * electric[0] + forward_f[1] * electric[1] + forward_f[2] * electric[2])
    padded_e = jnp.pad(electric, ((0, 0), (0, 1), (0, 1), (0, 1)))
    along_x = padded_e[:, 1:, :-1, :-1] - electric
    along_y = padded_e[:, :-1, 1:, :-1] - electric
    along_z = padded_e[:, :-1, :-1, 1:] - electric
    new_h = jnp.stack([magnetic[0] - COURANT * (along_y[2] - along_z[1]), magnetic[1] - COURANT * (along_z[0] - along_x[2]), magnetic[2] - COURANT * (along_x[1] - along_y[0])])
    padded_h = jnp.pad(new_h, ((0, 0), (1, 0), (1, 0), (1, 0)))
    back_x = new_h - padded_h[:, :-1, 1:, 1:]
    back_y = new_h - padded_h[:, 1:, :-1, 1:]
    back_z = new_h - padded_h[:, 1:, 1:, :-1]
    new_e = jnp.stack([keep_rate * electric[0] + drive_rate * (back_y[2] - back_z[1] + inject), keep_rate * electric[1] + drive_rate * (back_z[0] - back_x[2]), keep_rate * electric[2] + drive_rate * (back_x[1] - back_y[0])])
    return (jnp.concatenate([new_e, new_h], axis=0), panel)

def reference(adjoint_fields, forward_fields, rock_unit, unit_conductivity, receiver_cells, residuals, model_vectors):
    conductivity = unit_conductivity[rock_unit].astype(jnp.float32) * 0.001
    damping = LOSS_FACTOR * conductivity
    keep_rate = (1.0 - damping) / (1.0 + damping)
    drive_rate = COURANT / (1.0 + damping)
    cell_total = NX * NY * NZ

    def one_source(inputs):
        state, forward_src, residual_src = inputs
        panels = []
        for moment in range(STEPS):
            inject = jnp.zeros((cell_total,), jnp.float32).at[receiver_cells].add(residual_src[moment])
            state, panel = advance(state, forward_src[moment], conductivity, keep_rate, drive_rate, inject.reshape(NX, NY, NZ))
            panels.append(panel)
        return (state, jnp.stack(panels))
    states, panel_stack = lax.map(one_source, (jnp.moveaxis(adjoint_fields, 1, 0), jnp.moveaxis(forward_fields, 2, 0), jnp.moveaxis(residuals, 1, 0)))
    adjoint_state = jnp.moveaxis(states, 0, 1)
    panel_rows = jnp.moveaxis(panel_stack, 0, 1).reshape(STEPS * S, cell_total)
    vectors = jnp.moveaxis(model_vectors, 1, 0).reshape(NV, cell_total)
    weights = jnp.dot(panel_rows, vectors.T, precision=lax.Precision.HIGHEST)
    scale_factor = 1.0 / jnp.sqrt(jnp.float32(STEPS * S) * jnp.float32(cell_total))
    product = jnp.dot(weights.T, panel_rows, precision=lax.Precision.HIGHEST) * scale_factor
    normal_product = jnp.moveaxis(product.reshape(NV, NX, NY, NZ), 0, 1)
    return (adjoint_state, normal_product)
```

```python
import functools
import itertools
import math

import jax
import jax.numpy as jnp
from jax import lax
from jax.experimental import pallas as pl
from jax.experimental.pallas import tpu as pltpu
from jax.sharding import PartitionSpec as P

LOSS_FACTOR = 0.5
COURANT = 0.5
AXES = ("gx", "gy", "gz")
MESH = pl.DeviceIdType.MESH
ONE_STAGE_LIMIT = 64

E_LOW = ((-1, 0, 0), (0, -1, 0), (0, 0, -1))
H_HIGH = ((1, 0, 0), (0, 1, 0), (0, 0, 1))
LINES = ((1, 0, -1), (1, -1, 0), (-1, 1, 0), (0, 1, -1), (0, -1, 1), (-1, 0, 1))
TARGETS = E_LOW + H_HIGH + LINES


def reduce_stages(sizes):
    if math.prod(sizes) <= ONE_STAGE_LIMIT:
        return ((0, 1, 2),)
    return ((2,), (1,), (0,))


def stage_offsets(stage, sizes):
    ranges = [range(sizes[a]) if a in stage else range(1) for a in range(3)]
    return [o for o in itertools.product(*ranges) if any(o)]


def kernel(sizes, scale, fields, forward, rock, unit, cells, resid, model, state_out, normal_out,
           f0, fwd, rk, un, cl, rs, mv, st, fin, hp, xlow, xhigh, tx_buf, rx_buf, pan, nrm, *rest):
    stages = reduce_stages(sizes)
    stage_count = len(stages)
    msgs, gathers = rest[:stage_count], rest[stage_count:2 * stage_count]
    in_sem, out_sem, send_sem, recv_sem = rest[2 * stage_count:2 * stage_count + 4]
    sum_send, sum_recv = rest[2 * stage_count + 4:3 * stage_count + 4], rest[3 * stage_count + 4:]
    nx, ny, nz = rk.shape
    steps = fwd.shape[0]
    vectors = mv.shape[1]
    me = [lax.axis_index(a) for a in AXES]

    loads = [
        pltpu.make_async_copy(src, dst, in_sem.at[i])
        for i, (src, dst) in enumerate(
            ((fields, f0), (rock, rk), (unit, un), (forward, fwd), (model, mv), (cells, cl), (resid, rs))
        )
    ]
    for load in loads:
        load.start()

    def exists(offset):
        ok = None
        for a in range(3):
            if offset[a] == 0:
                continue
            here = (me[a] + offset[a] >= 0) & (me[a] + offset[a] < sizes[a])
            ok = here if ok is None else ok & here
        return ok

    def around(offset):
        return tuple(me[a] + offset[a] for a in range(3))

    def wrapped(offset):
        return tuple(
            me[a] if offset[a] == 0 else lax.rem(me[a] + offset[a], sizes[a]) for a in range(3)
        )

    barrier = pltpu.get_barrier_semaphore()
    expected = 0
    for stage in stages:
        for offset in stage_offsets(stage, sizes):
            pl.semaphore_signal(barrier, inc=1, device_id=wrapped(offset), device_id_type=MESH)
            expected = expected + 1
    if stage_count > 1:
        for offset in TARGETS:
            @pl.when(exists(offset))
            def _():
                pl.semaphore_signal(barrier, inc=1, device_id=around(offset), device_id_type=MESH)
            expected = expected + exists(offset).astype(jnp.int32)

    lane = lax.broadcasted_iota(jnp.int32, (ny, nz), 1)
    row = lax.broadcasted_iota(jnp.int32, (ny, nz), 0)
    zero = jnp.zeros((ny, nz), jnp.float32)
    last_x, last_y, last_z = nx - 1, ny - 1, nz - 1
    low_exists = [jnp.where(me[a] > 0, COURANT, 0.0).astype(jnp.float32) for a in range(3)]

    def up_y(f):
        return jnp.where(row == last_y, 0.0, pltpu.roll(f, last_y, 0))

    def up_z(f):
        return jnp.where(lane == last_z, 0.0, pltpu.roll(f, last_z, 1))

    def rows_of(ref, first, second, y):
        pack = zero
        for c, comp in enumerate((first, second)):
            if comp is None:
                continue
            for x in range(nx):
                pack = jnp.where(row == c * nx + x, jnp.broadcast_to(ref[comp, x, y:y + 1, :], (ny, nz)), pack)
        return pack

    def lanes_of(planes, z):
        pack = zero
        for i, plane in enumerate(planes):
            moved = pltpu.roll(plane, (i - z) % nz, 1) if (i - z) % nz else plane
            pack = jnp.where(lane == i, moved, pack)
        return pack

    def prepare(src, step):
        ex, ey, ez = ([src[c, x] for x in range(nx)] for c in range(3))
        for x in range(nx):
            ez_x = ez[x + 1] if x < last_x else zero
            ey_x = ey[x + 1] if x < last_x else zero
            hp[step, 0, x] = src[3, x] - COURANT * ((up_y(ez[x]) - ez[x]) - (up_z(ey[x]) - ey[x]))
            hp[step, 1, x] = src[4, x] - COURANT * ((up_z(ex[x]) - ex[x]) - (ez_x - ez[x]))
            hp[step, 2, x] = src[5, x] - COURANT * ((ey_x - ey[x]) - (up_y(ex[x]) - ex[x]))
        hps = hp.at[step]
        tx_buf[step, 0] = rows_of(src, 0, 2, 0)
        tx_buf[step, 1] = lanes_of(ey + ex, 0)
        tx_buf[step, 2] = rows_of(hps, 2, 0, last_y)
        tx_buf[step, 3] = lanes_of([hp[step, 0, x] for x in range(nx)] + [hp[step, 1, x] for x in range(nx)], last_z)
        tx_buf[step, 4] = jnp.where(lane == last_z, -COURANT * pltpu.roll(ex[last_x], last_z, 1), 0.0)
        tx_buf[step, 5] = jnp.where(row == last_y, COURANT * pltpu.roll(ex[last_x], last_y, 0), 0.0)
        tx_buf[step, 6] = jnp.where(
            row == last_x, -COURANT * jnp.broadcast_to(src[1, 0, last_y:last_y + 1, :], (ny, nz)), 0.0
        )
        tx_buf[step, 7] = jnp.where(
            lane == last_z, COURANT * pltpu.roll(rows_of(src, None, 1, last_y), last_z, 1), 0.0
        )
        tx_buf[step, 8] = jnp.where(row == last_y, -COURANT * pltpu.roll(lanes_of(ez, last_z), last_y, 0), 0.0)
        at = 2 * nx - 1
        tx_buf[step, 9] = jnp.where(lane == at, COURANT * pltpu.roll(ez[0], (at - last_z) % nz, 1), 0.0)

    def halo_copy(src, step, i):
        if i == 0:
            source, target = src.at[pl.ds(1, 2), 0], xlow.at[step]
        elif i == 3:
            source, target = hp.at[step, pl.ds(1, 2), last_x], xhigh.at[step]
        else:
            slot = i - 1 if i < 3 else i - 2
            source, target = tx_buf.at[step, slot], rx_buf.at[step, slot]
        return pltpu.make_async_remote_copy(
            src_ref=source, dst_ref=target, send_sem=send_sem.at[step, i], recv_sem=recv_sem.at[step, i],
            device_id=around(TARGETS[i]), device_id_type=MESH,
        )

    def send(src, step):
        for i in range(12):
            @pl.when(exists(TARGETS[i]))
            def _():
                halo_copy(src, step, i).start()

    def receive(src, step):
        for i in range(12):
            source = exists(tuple(-d for d in TARGETS[i]))

            @pl.when(source)
            def _():
                halo_copy(src, step, i).wait_recv()

            @pl.when(jnp.logical_not(source))
            def _():
                if i == 0:
                    xlow[step] = jnp.zeros(xlow.shape[1:], jnp.float32)
                elif i == 3:
                    xhigh[step] = jnp.zeros(xhigh.shape[1:], jnp.float32)
                else:
                    rx_buf[step, i - 1 if i < 3 else i - 2] = zero

    def sent(src, step):
        for i in range(12):
            @pl.when(exists(TARGETS[i]))
            def _():
                halo_copy(src, step, i).wait_send()

    def advance(src, dst, step, keep, drive, inject):
        y_high = lambda r: jnp.broadcast_to(rx_buf[step, 0, r:r + 1, :], (ny, nz))
        z_pack = rx_buf[step, 1]
        hx, hy, hz = [], [], []
        half = jnp.float32(COURANT)
        for x in range(nx):
            z_of = lambda l: jnp.where(lane == last_z, half * pltpu.roll(z_pack, last_z - l, 1), 0.0)
            y_of = lambda r: jnp.where(row == last_y, half * y_high(r), 0.0)
            hx.append(hp[step, 0, x] + z_of(x) - y_of(nx + x))
            hy.append(hp[step, 1, x] - z_of(nx + x))
            hz.append(hp[step, 2, x] + y_of(x))
        hy[last_x] = hy[last_x] + half * xlow[step, 1]
        hz[last_x] = hz[last_x] - half * xlow[step, 0]
        for x in range(nx):
            dst[3, x], dst[4, x], dst[5, x] = hx[x], hy[x], hz[x]
        hy_x = xhigh[step, 0] + low_exists[0] * src[2, 0] + rx_buf[step, 4]
        hz_x = xhigh[step, 1] - low_exists[0] * src[1, 0] + rx_buf[step, 5]
        y_sign = jnp.where(row < nx, low_exists[1], -low_exists[1])
        z_sign = jnp.where(lane < nx, low_exists[2], -low_exists[2])
        h_y = rx_buf[step, 2] + y_sign * tx_buf[step, 0] + rx_buf[step, 6] + rx_buf[step, 7]
        h_z = rx_buf[step, 3] + z_sign * tx_buf[step, 1] + rx_buf[step, 8] + rx_buf[step, 9]

        def back_y(h, r):
            return h - jnp.where(row == 0, jnp.broadcast_to(h_y[r:r + 1, :], (ny, nz)), pltpu.roll(h, 1, 0))

        def back_z(h, l):
            below = pltpu.roll(h_z, (nz - l) % nz, 1) if l else h_z
            return h - jnp.where(lane == 0, below, pltpu.roll(h, 1, 1))

        for x in range(nx):
            dst[0, x] = keep[x] * src[0, x] + drive[x] * (
                back_y(hz[x], x) - back_z(hy[x], nx + x) + inject[x]
            )
            back_x = hz[x] - (hz[x - 1] if x else hz_x)
            dst[1, x] = keep[x] * src[1, x] + drive[x] * (back_z(hx[x], x) - back_x)
            back_x = hy[x] - (hy[x - 1] if x else hy_x)
            dst[2, x] = keep[x] * src[2, x] + drive[x] * (back_x - back_y(hx[x], nx + x))

    def panel_of(src, step, sigma):
        sums = [zero] * vectors
        for x in range(nx):
            p = sigma[x] * (
                fwd[step, 0, x].astype(jnp.float32) * src[0, x]
                + fwd[step, 1, x].astype(jnp.float32) * src[1, x]
                + fwd[step, 2, x].astype(jnp.float32) * src[2, x]
            )
            pan[step, x] = p
            sums = [s + p * mv[x, n] for n, s in enumerate(sums)]
        message = jnp.zeros((1, nz), jnp.float32)
        one_row = lax.broadcasted_iota(jnp.int32, (1, nz), 1)
        for n in range(vectors):
            total = jnp.sum(jnp.sum(sums[n], axis=0, keepdims=True), axis=1, keepdims=True)
            message = jnp.where(one_row == step * vectors + n, total, message)
        return message

    loads[0].wait()
    prepare(f0, 0)
    pl.semaphore_wait(barrier, expected)
    send(f0, 0)

    for load in loads[1:]:
        load.wait()
    sigma, keep, drive = [], [], []
    for x in range(nx):
        found = jnp.zeros((ny, nz), jnp.int32)
        units = rk[x]
        for u in range(unit.shape[0]):
            found = jnp.where(units == u, un[u], found)
        s = found.astype(jnp.float32) * 0.001
        damping = LOSS_FACTOR * s
        sigma.append(s)
        keep.append((1.0 - damping) / (1.0 + damping))
        drive.append(COURANT / (1.0 + damping))

    count = cl.shape[1]
    at = lax.broadcasted_iota(jnp.int32, (nx * ny, count), 0)
    line = (me[0] * nx + at // ny) * (sizes[1] * ny) + me[1] * ny + at % ny
    start = line * (sizes[2] * nz) + me[2] * nz
    where_cells = cl[...]
    in_row = (where_cells >= start) & (where_cells < start + nz)
    spikes = jnp.concatenate([jnp.where(in_row, rs[t], 0.0) for t in range(steps)], axis=0)
    place = lax.broadcasted_iota(jnp.int32, (nz, count), 0)
    hits = jnp.where(place == lax.rem(where_cells, nz), 1.0, 0.0)
    injected = lax.dot_general(
        spikes, hits, (((1,), (1,)), ((), ())), precision=lax.Precision.HIGHEST,
        preferred_element_type=jnp.float32,
    )
    inject = [
        [injected[(t * nx + x) * ny:(t * nx + x + 1) * ny] for x in range(nx)] for t in range(steps)
    ]
    message = panel_of(f0, 0, sigma)

    source = f0
    for step in range(steps):
        target = fin if step == steps - 1 else st.at[step]
        if step > 0:
            message = message + panel_of(source, step, sigma)
            if step == steps - 1:
                msgs[0][...] = message
                for i, offset in enumerate(stage_offsets(stages[0], sizes)):
                    sum_copy(msgs[0], gathers[0], sum_send[0], sum_recv[0], i, wrapped(offset)).start()
            prepare(source, step)
            send(source, step)
        receive(source, step)
        advance(source, target, step, keep, drive, inject[step])
        source = target
    out_state = pltpu.make_async_copy(fin, state_out, out_sem.at[0])
    out_state.start()

    for s, stage in enumerate(stages):
        offsets = stage_offsets(stage, sizes)
        if s > 0:
            msgs[s][...] = message
            for i, offset in enumerate(offsets):
                sum_copy(msgs[s], gathers[s], sum_send[s], sum_recv[s], i, wrapped(offset)).start()
        for i, offset in enumerate(offsets):
            sum_copy(msgs[s], gathers[s], sum_send[s], sum_recv[s], i, wrapped(offset)).wait_recv()
        for i in range(len(offsets)):
            message = message + gathers[s][i]
    weights = [
        [
            jnp.broadcast_to(message[:, k * vectors + n:k * vectors + n + 1] * scale, (ny, nz))
            for n in range(vectors)
        ]
        for k in range(steps)
    ]
    for x in range(nx):
        for n in range(vectors):
            total = pan[0, x] * weights[0][n]
            for k in range(1, steps):
                total = total + pan[k, x] * weights[k][n]
            nrm[x, n] = total
    out_normal = pltpu.make_async_copy(nrm, normal_out, out_sem.at[1])
    out_normal.start()

    for step in range(steps):
        sent(f0 if step == 0 else st.at[step - 1], step)
    for s, stage in enumerate(stages):
        for i, offset in enumerate(stage_offsets(stage, sizes)):
            sum_copy(msgs[s], gathers[s], sum_send[s], sum_recv[s], i, wrapped(offset)).wait_send()
    out_state.wait()
    out_normal.wait()


def sum_copy(source, target, send, recv, i, device):
    return pltpu.make_async_remote_copy(
        src_ref=source, dst_ref=target.at[i], send_sem=send.at[i], recv_sem=recv.at[i],
        device_id=device, device_id_type=MESH,
    )


def local(sizes, adjoint_fields, forward_fields, rock_unit, unit_conductivity, receiver_cells, residuals, model_vectors):
    steps = forward_fields.shape[0]
    nx, ny, nz = rock_unit.shape
    units = unit_conductivity.shape[0]
    receivers = receiver_cells.shape[0]
    vectors = model_vectors.shape[1]
    assert adjoint_fields.shape[1] == 1 and 2 * nx <= ny and steps * vectors <= nz
    cell_total = nx * ny * nz * math.prod(sizes)
    scale = 1.0 / math.sqrt(float(steps) * float(cell_total))
    fields = adjoint_fields.reshape(6, nx, ny, nz)
    forward = forward_fields.reshape(steps, 3, nx, ny, nz)
    cells = receiver_cells.reshape(1, receivers)
    stages = reduce_stages(sizes)
    counts = [len(stage_offsets(stage, sizes)) for stage in stages]
    f32 = jnp.float32
    scratch = [
        pltpu.VMEM((6, nx, ny, nz), f32),
        pltpu.VMEM(forward.shape, forward.dtype),
        pltpu.VMEM((nx, ny, nz), jnp.int32),
        pltpu.SMEM((units,), jnp.int32),
        pltpu.VMEM((1, receivers), jnp.int32),
        pltpu.VMEM(residuals.shape, f32),
        pltpu.VMEM(model_vectors.shape, f32),
        pltpu.VMEM((max(steps - 1, 1), 6, nx, ny, nz), f32),
        pltpu.VMEM((6, nx, ny, nz), f32),
        pltpu.VMEM((steps, 3, nx, ny, nz), f32),
        pltpu.VMEM((steps, 2, ny, nz), f32),
        pltpu.VMEM((steps, 2, ny, nz), f32),
        pltpu.VMEM((steps, 10, ny, nz), f32),
        pltpu.VMEM((steps, 10, ny, nz), f32),
        pltpu.VMEM((steps, nx, ny, nz), f32),
        pltpu.VMEM(model_vectors.shape, f32),
        *[pltpu.VMEM((1, nz), f32) for _ in stages],
        *[pltpu.VMEM((count, 1, nz), f32) for count in counts],
        pltpu.SemaphoreType.DMA((7,)),
        pltpu.SemaphoreType.DMA((2,)),
        pltpu.SemaphoreType.DMA((steps, 12)),
        pltpu.SemaphoreType.DMA((steps, 12)),
        *[pltpu.SemaphoreType.DMA((count,)) for count in counts],
        *[pltpu.SemaphoreType.DMA((count,)) for count in counts],
    ]
    anywhere = pl.BlockSpec(memory_space=pl.ANY)
    state, normal = pl.pallas_call(
        functools.partial(kernel, sizes, scale),
        out_shape=(
            jax.ShapeDtypeStruct(fields.shape, f32),
            jax.ShapeDtypeStruct(model_vectors.shape, f32),
        ),
        in_specs=[anywhere] * 7,
        out_specs=(anywhere, anywhere),
        scratch_shapes=scratch,
        compiler_params=pltpu.CompilerParams(
            collective_id=0, has_side_effects=True, vmem_limit_bytes=16 * 2**20
        ),
    )(fields, forward, rock_unit, unit_conductivity, cells, residuals, model_vectors)
    return state.reshape(adjoint_fields.shape), normal


def solution(mesh):
    sizes = tuple(mesh.shape[a] for a in AXES)
    in_specs = (
        P(None, None, "gx", "gy", "gz"),
        P(None, None, None, "gx", "gy", "gz"),
        P("gx", "gy", "gz"),
        P(),
        P(),
        P(),
        P("gx", None, "gy", "gz"),
    )
    out_specs = (P(None, None, "gx", "gy", "gz"), P("gx", None, "gy", "gz"))
    return jax.shard_map(
        functools.partial(local, sizes), mesh=mesh, in_specs=in_specs, out_specs=out_specs, check_vma=False
    )
```

```python
import functools
import itertools
import math

import jax
import jax.numpy as jnp
from jax import lax
from jax.experimental import pallas as pl
from jax.experimental.pallas import tpu as pltpu
from jax.sharding import PartitionSpec as P

LOSS_FACTOR = 0.5
COURANT = 0.5
AXES = ("gx", "gy", "gz")
MESH = pl.DeviceIdType.MESH
ONE_STAGE_LIMIT = 64

E_LOW = ((-1, 0, 0), (0, -1, 0), (0, 0, -1))
H_HIGH = ((1, 0, 0), (0, 1, 0), (0, 0, 1))
LINES = ((1, 0, -1), (1, -1, 0), (-1, 1, 0), (0, 1, -1), (0, -1, 1), (-1, 0, 1))
TARGETS = E_LOW + H_HIGH + LINES


def reduce_stages(sizes):
    if math.prod(sizes) <= ONE_STAGE_LIMIT:
        return ((0, 1, 2),)
    return ((2,), (1,), (0,))


def stage_offsets(stage, sizes):
    ranges = [range(sizes[a]) if a in stage else range(1) for a in range(3)]
    return [o for o in itertools.product(*ranges) if any(o)]


def kernel(sizes, fields, forward, rock, unit, cells, resid, model, fin, pan, weights,
           f0, fwd, rk, un, cl, rs, mv, st, hp, xlow, xhigh, tx_buf, rx_buf, *rest):
    stages = reduce_stages(sizes)
    stage_count = len(stages)
    msgs, gathers = rest[:stage_count], rest[stage_count:2 * stage_count]
    in_sem, send_sem, recv_sem = rest[2 * stage_count:2 * stage_count + 3]
    sum_send, sum_recv = rest[2 * stage_count + 3:3 * stage_count + 3], rest[3 * stage_count + 3:]
    nx, ny, nz = rk.shape
    steps = fwd.shape[0]
    vectors = mv.shape[1]
    me = [lax.axis_index(a) for a in AXES]

    loads = [
        pltpu.make_async_copy(src, dst, in_sem.at[i])
        for i, (src, dst) in enumerate(
            ((fields, f0), (rock, rk), (unit, un), (forward, fwd), (model, mv), (cells, cl), (resid, rs))
        )
    ]
    for load in loads:
        load.start()

    def exists(offset):
        ok = None
        for a in range(3):
            if offset[a] == 0:
                continue
            here = (me[a] + offset[a] >= 0) & (me[a] + offset[a] < sizes[a])
            ok = here if ok is None else ok & here
        return ok

    def around(offset):
        return tuple(me[a] + offset[a] for a in range(3))

    def wrapped(offset):
        return tuple(
            me[a] if offset[a] == 0 else lax.rem(me[a] + offset[a], sizes[a]) for a in range(3)
        )

    barrier = pltpu.get_barrier_semaphore()
    expected = 0
    for stage in stages:
        for offset in stage_offsets(stage, sizes):
            pl.semaphore_signal(barrier, inc=1, device_id=wrapped(offset), device_id_type=MESH)
            expected = expected + 1
    if stage_count > 1:
        for offset in TARGETS:
            @pl.when(exists(offset))
            def _():
                pl.semaphore_signal(barrier, inc=1, device_id=around(offset), device_id_type=MESH)
            expected = expected + exists(offset).astype(jnp.int32)

    lane = lax.broadcasted_iota(jnp.int32, (ny, nz), 1)
    row = lax.broadcasted_iota(jnp.int32, (ny, nz), 0)
    zero = jnp.zeros((ny, nz), jnp.float32)
    last_x, last_y, last_z = nx - 1, ny - 1, nz - 1
    low_exists = [jnp.where(me[a] > 0, COURANT, 0.0).astype(jnp.float32) for a in range(3)]

    def up_y(f):
        return jnp.where(row == last_y, 0.0, pltpu.roll(f, last_y, 0))

    def up_z(f):
        return jnp.where(lane == last_z, 0.0, pltpu.roll(f, last_z, 1))

    def rows_of(ref, first, second, y):
        pack = zero
        for c, comp in enumerate((first, second)):
            if comp is None:
                continue
            for x in range(nx):
                pack = jnp.where(row == c * nx + x, jnp.broadcast_to(ref[comp, x, y:y + 1, :], (ny, nz)), pack)
        return pack

    def lanes_of(planes, z):
        pack = zero
        for i, plane in enumerate(planes):
            moved = pltpu.roll(plane, (i - z) % nz, 1) if (i - z) % nz else plane
            pack = jnp.where(lane == i, moved, pack)
        return pack

    def prepare(src, step):
        ex, ey, ez = ([src[c, x] for x in range(nx)] for c in range(3))
        for x in range(nx):
            ez_x = ez[x + 1] if x < last_x else zero
            ey_x = ey[x + 1] if x < last_x else zero
            hp[step, 0, x] = src[3, x] - COURANT * ((up_y(ez[x]) - ez[x]) - (up_z(ey[x]) - ey[x]))
            hp[step, 1, x] = src[4, x] - COURANT * ((up_z(ex[x]) - ex[x]) - (ez_x - ez[x]))
            hp[step, 2, x] = src[5, x] - COURANT * ((ey_x - ey[x]) - (up_y(ex[x]) - ex[x]))
        hps = hp.at[step]
        tx_buf[step, 0] = rows_of(src, 0, 2, 0)
        tx_buf[step, 1] = lanes_of(ey + ex, 0)
        tx_buf[step, 2] = rows_of(hps, 2, 0, last_y)
        tx_buf[step, 3] = lanes_of([hp[step, 0, x] for x in range(nx)] + [hp[step, 1, x] for x in range(nx)], last_z)
        tx_buf[step, 4] = jnp.where(lane == last_z, -COURANT * pltpu.roll(ex[last_x], last_z, 1), 0.0)
        tx_buf[step, 5] = jnp.where(row == last_y, COURANT * pltpu.roll(ex[last_x], last_y, 0), 0.0)
        tx_buf[step, 6] = jnp.where(
            row == last_x, -COURANT * jnp.broadcast_to(src[1, 0, last_y:last_y + 1, :], (ny, nz)), 0.0
        )
        tx_buf[step, 7] = jnp.where(
            lane == last_z, COURANT * pltpu.roll(rows_of(src, None, 1, last_y), last_z, 1), 0.0
        )
        tx_buf[step, 8] = jnp.where(row == last_y, -COURANT * pltpu.roll(lanes_of(ez, last_z), last_y, 0), 0.0)
        at = 2 * nx - 1
        tx_buf[step, 9] = jnp.where(lane == at, COURANT * pltpu.roll(ez[0], (at - last_z) % nz, 1), 0.0)

    def halo_copy(src, step, i):
        if i == 0:
            source, target = src.at[pl.ds(1, 2), 0], xlow.at[step]
        elif i == 3:
            source, target = hp.at[step, pl.ds(1, 2), last_x], xhigh.at[step]
        else:
            slot = i - 1 if i < 3 else i - 2
            source, target = tx_buf.at[step, slot], rx_buf.at[step, slot]
        return pltpu.make_async_remote_copy(
            src_ref=source, dst_ref=target, send_sem=send_sem.at[step, i], recv_sem=recv_sem.at[step, i],
            device_id=around(TARGETS[i]), device_id_type=MESH,
        )

    def send(src, step):
        for i in range(12):
            @pl.when(exists(TARGETS[i]))
            def _():
                halo_copy(src, step, i).start()

    def receive(src, step):
        for i in range(12):
            source = exists(tuple(-d for d in TARGETS[i]))

            @pl.when(source)
            def _():
                halo_copy(src, step, i).wait_recv()

            @pl.when(jnp.logical_not(source))
            def _():
                if i == 0:
                    xlow[step] = jnp.zeros(xlow.shape[1:], jnp.float32)
                elif i == 3:
                    xhigh[step] = jnp.zeros(xhigh.shape[1:], jnp.float32)
                else:
                    rx_buf[step, i - 1 if i < 3 else i - 2] = zero

    def sent(src, step):
        for i in range(12):
            @pl.when(exists(TARGETS[i]))
            def _():
                halo_copy(src, step, i).wait_send()

    def advance(src, dst, step, keep, drive, inject):
        y_high = lambda r: jnp.broadcast_to(rx_buf[step, 0, r:r + 1, :], (ny, nz))
        z_pack = rx_buf[step, 1]
        hx, hy, hz = [], [], []
        half = jnp.float32(COURANT)
        for x in range(nx):
            z_of = lambda l: jnp.where(lane == last_z, half * pltpu.roll(z_pack, last_z - l, 1), 0.0)
            y_of = lambda r: jnp.where(row == last_y, half * y_high(r), 0.0)
            hx.append(hp[step, 0, x] + z_of(x) - y_of(nx + x))
            hy.append(hp[step, 1, x] - z_of(nx + x))
            hz.append(hp[step, 2, x] + y_of(x))
        hy[last_x] = hy[last_x] + half * xlow[step, 1]
        hz[last_x] = hz[last_x] - half * xlow[step, 0]
        for x in range(nx):
            dst[3, x], dst[4, x], dst[5, x] = hx[x], hy[x], hz[x]
        hy_x = xhigh[step, 0] + low_exists[0] * src[2, 0] + rx_buf[step, 4]
        hz_x = xhigh[step, 1] - low_exists[0] * src[1, 0] + rx_buf[step, 5]
        y_sign = jnp.where(row < nx, low_exists[1], -low_exists[1])
        z_sign = jnp.where(lane < nx, low_exists[2], -low_exists[2])
        h_y = rx_buf[step, 2] + y_sign * tx_buf[step, 0] + rx_buf[step, 6] + rx_buf[step, 7]
        h_z = rx_buf[step, 3] + z_sign * tx_buf[step, 1] + rx_buf[step, 8] + rx_buf[step, 9]

        def back_y(h, r):
            return h - jnp.where(row == 0, jnp.broadcast_to(h_y[r:r + 1, :], (ny, nz)), pltpu.roll(h, 1, 0))

        def back_z(h, l):
            below = pltpu.roll(h_z, (nz - l) % nz, 1) if l else h_z
            return h - jnp.where(lane == 0, below, pltpu.roll(h, 1, 1))

        for x in range(nx):
            dst[0, x] = keep[x] * src[0, x] + drive[x] * (
                back_y(hz[x], x) - back_z(hy[x], nx + x) + inject[x]
            )
            back_x = hz[x] - (hz[x - 1] if x else hz_x)
            dst[1, x] = keep[x] * src[1, x] + drive[x] * (back_z(hx[x], x) - back_x)
            back_x = hy[x] - (hy[x - 1] if x else hy_x)
            dst[2, x] = keep[x] * src[2, x] + drive[x] * (back_x - back_y(hx[x], nx + x))

    def panel_of(src, step, sigma):
        sums = [zero] * vectors
        for x in range(nx):
            p = sigma[x] * (
                fwd[step, 0, x].astype(jnp.float32) * src[0, x]
                + fwd[step, 1, x].astype(jnp.float32) * src[1, x]
                + fwd[step, 2, x].astype(jnp.float32) * src[2, x]
            )
            pan[step, x] = p
            sums = [s + p * mv[x, n] for n, s in enumerate(sums)]
        message = jnp.zeros((1, nz), jnp.float32)
        one_row = lax.broadcasted_iota(jnp.int32, (1, nz), 1)
        for n in range(vectors):
            total = jnp.sum(jnp.sum(sums[n], axis=0, keepdims=True), axis=1, keepdims=True)
            message = jnp.where(one_row == step * vectors + n, total, message)
        return message

    loads[0].wait()
    prepare(f0, 0)
    pl.semaphore_wait(barrier, expected)
    send(f0, 0)

    for load in loads[1:]:
        load.wait()
    sigma, keep, drive = [], [], []
    for x in range(nx):
        found = jnp.zeros((ny, nz), jnp.int32)
        units = rk[x]
        for u in range(unit.shape[0]):
            found = jnp.where(units == u, un[u], found)
        s = found.astype(jnp.float32) * 0.001
        damping = LOSS_FACTOR * s
        sigma.append(s)
        keep.append((1.0 - damping) / (1.0 + damping))
        drive.append(COURANT / (1.0 + damping))

    count = cl.shape[1]
    at = lax.broadcasted_iota(jnp.int32, (nx * ny, count), 0)
    line = (me[0] * nx + at // ny) * (sizes[1] * ny) + me[1] * ny + at % ny
    start = line * (sizes[2] * nz) + me[2] * nz
    where_cells = cl[...]
    in_row = (where_cells >= start) & (where_cells < start + nz)
    spikes = jnp.concatenate([jnp.where(in_row, rs[t], 0.0) for t in range(steps)], axis=0)
    place = lax.broadcasted_iota(jnp.int32, (nz, count), 0)
    hits = jnp.where(place == lax.rem(where_cells, nz), 1.0, 0.0)
    injected = lax.dot_general(
        spikes, hits, (((1,), (1,)), ((), ())), precision=lax.Precision.HIGHEST,
        preferred_element_type=jnp.float32,
    )
    inject = [
        [injected[(t * nx + x) * ny:(t * nx + x + 1) * ny] for x in range(nx)] for t in range(steps)
    ]
    message = panel_of(f0, 0, sigma)

    source = f0
    for step in range(steps):
        target = fin if step == steps - 1 else st.at[step]
        if step > 0:
            message = message + panel_of(source, step, sigma)
            if step == steps - 1:
                msgs[0][...] = message
                for i, offset in enumerate(stage_offsets(stages[0], sizes)):
                    sum_copy(msgs[0], gathers[0], sum_send[0], sum_recv[0], i, wrapped(offset)).start()
            prepare(source, step)
            send(source, step)
        receive(source, step)
        advance(source, target, step, keep, drive, inject[step])
        source = target

    for s, stage in enumerate(stages):
        offsets = stage_offsets(stage, sizes)
        if s > 0:
            msgs[s][...] = message
            for i, offset in enumerate(offsets):
                sum_copy(msgs[s], gathers[s], sum_send[s], sum_recv[s], i, wrapped(offset)).start()
        for i, offset in enumerate(offsets):
            sum_copy(msgs[s], gathers[s], sum_send[s], sum_recv[s], i, wrapped(offset)).wait_recv()
        for i in range(len(offsets)):
            message = message + gathers[s][i]
    weights[...] = message

    for step in range(steps):
        sent(f0 if step == 0 else st.at[step - 1], step)
    for s, stage in enumerate(stages):
        for i, offset in enumerate(stage_offsets(stage, sizes)):
            sum_copy(msgs[s], gathers[s], sum_send[s], sum_recv[s], i, wrapped(offset)).wait_send()


def finish(scale, state, pan, weights, state_out, normal_out, nrm, out_sem):
    out_state = pltpu.make_async_copy(state, state_out, out_sem.at[0])
    out_state.start()
    steps, nx, ny, nz = pan.shape
    vectors = nrm.shape[1]
    message = weights[...] * scale
    spread = [jnp.broadcast_to(message[:, i:i + 1], (ny, nz)) for i in range(steps * vectors)]
    for x in range(nx):
        for n in range(vectors):
            total = pan[0, x] * spread[n]
            for k in range(1, steps):
                total = total + pan[k, x] * spread[k * vectors + n]
            nrm[x, n] = total
    out_normal = pltpu.make_async_copy(nrm, normal_out, out_sem.at[1])
    out_normal.start()
    out_state.wait()
    out_normal.wait()


def sum_copy(source, target, send, recv, i, device):
    return pltpu.make_async_remote_copy(
        src_ref=source, dst_ref=target.at[i], send_sem=send.at[i], recv_sem=recv.at[i],
        device_id=device, device_id_type=MESH,
    )


def local(sizes, adjoint_fields, forward_fields, rock_unit, unit_conductivity, receiver_cells, residuals, model_vectors):
    steps = forward_fields.shape[0]
    nx, ny, nz = rock_unit.shape
    units = unit_conductivity.shape[0]
    receivers = receiver_cells.shape[0]
    vectors = model_vectors.shape[1]
    assert adjoint_fields.shape[1] == 1 and 2 * nx <= ny and steps * vectors <= nz
    cell_total = nx * ny * nz * math.prod(sizes)
    scale = 1.0 / math.sqrt(float(steps) * float(cell_total))
    fields = adjoint_fields.reshape(6, nx, ny, nz)
    forward = forward_fields.reshape(steps, 3, nx, ny, nz)
    cells = receiver_cells.reshape(1, receivers)
    stages = reduce_stages(sizes)
    counts = [len(stage_offsets(stage, sizes)) for stage in stages]
    f32 = jnp.float32
    scratch = [
        pltpu.VMEM((6, nx, ny, nz), f32),
        pltpu.VMEM(forward.shape, forward.dtype),
        pltpu.VMEM((nx, ny, nz), jnp.int32),
        pltpu.SMEM((units,), jnp.int32),
        pltpu.VMEM((1, receivers), jnp.int32),
        pltpu.VMEM(residuals.shape, f32),
        pltpu.VMEM(model_vectors.shape, f32),
        pltpu.VMEM((max(steps - 1, 1), 6, nx, ny, nz), f32),
        pltpu.VMEM((steps, 3, nx, ny, nz), f32),
        pltpu.VMEM((steps, 2, ny, nz), f32),
        pltpu.VMEM((steps, 2, ny, nz), f32),
        pltpu.VMEM((steps, 10, ny, nz), f32),
        pltpu.VMEM((steps, 10, ny, nz), f32),
        *[pltpu.VMEM((1, nz), f32) for _ in stages],
        *[pltpu.VMEM((count, 1, nz), f32) for count in counts],
        pltpu.SemaphoreType.DMA((7,)),
        pltpu.SemaphoreType.DMA((steps, 12)),
        pltpu.SemaphoreType.DMA((steps, 12)),
        *[pltpu.SemaphoreType.DMA((count,)) for count in counts],
        *[pltpu.SemaphoreType.DMA((count,)) for count in counts],
    ]
    hbm = pl.BlockSpec(memory_space=pltpu.HBM)
    vmem = pl.BlockSpec(memory_space=pltpu.VMEM)
    state, panel, weights = pl.pallas_call(
        functools.partial(kernel, sizes),
        out_shape=(
            pltpu.VMEM(fields.shape, f32),
            pltpu.VMEM((steps, nx, ny, nz), f32),
            pltpu.VMEM((1, nz), f32),
        ),
        in_specs=[hbm] * 7,
        out_specs=(vmem, vmem, vmem),
        scratch_shapes=scratch,
        compiler_params=pltpu.CompilerParams(
            collective_id=0, has_side_effects=True, vmem_limit_bytes=60 * 2**20
        ),
    )(fields, forward, rock_unit, unit_conductivity, cells, residuals, model_vectors)
    state, normal = pl.pallas_call(
        functools.partial(finish, scale),
        out_shape=(
            jax.ShapeDtypeStruct(fields.shape, f32),
            jax.ShapeDtypeStruct(model_vectors.shape, f32),
        ),
        in_specs=[vmem, vmem, vmem],
        out_specs=(hbm, hbm),
        scratch_shapes=[pltpu.VMEM(model_vectors.shape, f32), pltpu.SemaphoreType.DMA((2,))],
        compiler_params=pltpu.CompilerParams(vmem_limit_bytes=16 * 2**20),
    )(state, panel, weights)
    return state.reshape(adjoint_fields.shape), normal


def solution(mesh):
    sizes = tuple(mesh.shape[a] for a in AXES)
    in_specs = (
        P(None, None, "gx", "gy", "gz"),
        P(None, None, None, "gx", "gy", "gz"),
        P("gx", "gy", "gz"),
        P(),
        P(),
        P(),
        P("gx", None, "gy", "gz"),
    )
    out_specs = (P(None, None, "gx", "gy", "gz"), P("gx", None, "gy", "gz"))
    return jax.shard_map(
        functools.partial(local, sizes), mesh=mesh, in_specs=in_specs, out_specs=out_specs, check_vma=False
    )
```

```python
import functools
import itertools
import math

import jax
import jax.numpy as jnp
from jax import lax
from jax.experimental import pallas as pl
from jax.experimental.pallas import tpu as pltpu
from jax.sharding import PartitionSpec as P

LOSS_FACTOR = 0.5
COURANT = 0.5
AXES = ("gx", "gy", "gz")
MESH = pl.DeviceIdType.MESH
ONE_STAGE_LIMIT = 64

E_LOW = ((-1, 0, 0), (0, -1, 0), (0, 0, -1))
H_HIGH = ((1, 0, 0), (0, 1, 0), (0, 0, 1))
LINES = ((1, 0, -1), (1, -1, 0), (-1, 1, 0), (0, 1, -1), (0, -1, 1), (-1, 0, 1))
TARGETS = E_LOW + H_HIGH + LINES
E_FIRST, H_NEXT = (6, 7, 8, 9, 10, 11, 0, 1, 2), (3, 4, 5)


def reduce_stages(sizes):
    if math.prod(sizes) <= ONE_STAGE_LIMIT:
        return ((0, 1, 2),)
    return ((2,), (1,), (0,))


def stage_offsets(stage, sizes):
    ranges = [range(sizes[a]) if a in stage else range(1) for a in range(3)]
    return [o for o in itertools.product(*ranges) if any(o)][::-1]


def kernel(sizes, fields, forward, rock, unit, cells, resid, model, fin, pan, weights,
           f0, fwd, rk, un, cl, rs, mv, st, hp, xlow, xhigh, tx_buf, rx_buf, *rest):
    stages = reduce_stages(sizes)
    stage_count = len(stages)
    msgs, gathers = rest[:stage_count], rest[stage_count:2 * stage_count]
    in_sem, send_sem, recv_sem = rest[2 * stage_count:2 * stage_count + 3]
    sum_send, sum_recv = rest[2 * stage_count + 3:3 * stage_count + 3], rest[3 * stage_count + 3:]
    nx, ny, nz = rk.shape
    steps = fwd.shape[0]
    vectors = mv.shape[1]
    me = [lax.axis_index(a) for a in AXES]

    loads = [
        pltpu.make_async_copy(src, dst, in_sem.at[i])
        for i, (src, dst) in enumerate(
            ((fields, f0), (rock, rk), (unit, un), (forward, fwd), (model, mv), (cells, cl), (resid, rs))
        )
    ]
    for load in loads:
        load.start()

    def exists(offset):
        ok = None
        for a in range(3):
            if offset[a] == 0:
                continue
            here = (me[a] + offset[a] >= 0) & (me[a] + offset[a] < sizes[a])
            ok = here if ok is None else ok & here
        return ok

    def around(offset):
        return tuple(me[a] + offset[a] for a in range(3))

    def wrapped(offset):
        return tuple(
            me[a] if offset[a] == 0 else lax.rem(me[a] + offset[a], sizes[a]) for a in range(3)
        )

    barrier = pltpu.get_barrier_semaphore()
    expected = 0
    for stage in stages:
        for offset in stage_offsets(stage, sizes):
            pl.semaphore_signal(barrier, inc=1, device_id=wrapped(offset), device_id_type=MESH)
            expected = expected + 1
    if stage_count > 1:
        for offset in TARGETS:
            @pl.when(exists(offset))
            def _():
                pl.semaphore_signal(barrier, inc=1, device_id=around(offset), device_id_type=MESH)
            expected = expected + exists(offset).astype(jnp.int32)

    lane = lax.broadcasted_iota(jnp.int32, (ny, nz), 1)
    row = lax.broadcasted_iota(jnp.int32, (ny, nz), 0)
    zero = jnp.zeros((ny, nz), jnp.float32)
    last_x, last_y, last_z = nx - 1, ny - 1, nz - 1
    low_exists = [jnp.where(me[a] > 0, COURANT, 0.0).astype(jnp.float32) for a in range(3)]

    def up_y(f):
        return jnp.where(row == last_y, 0.0, pltpu.roll(f, last_y, 0))

    def up_z(f):
        return jnp.where(lane == last_z, 0.0, pltpu.roll(f, last_z, 1))

    def rows_of(ref, first, second, y):
        pack = zero
        for c, comp in enumerate((first, second)):
            if comp is None:
                continue
            for x in range(nx):
                pack = jnp.where(row == c * nx + x, jnp.broadcast_to(ref[comp, x, y:y + 1, :], (ny, nz)), pack)
        return pack

    def lanes_of(planes, z):
        pack = zero
        for i, plane in enumerate(planes):
            moved = pltpu.roll(plane, (i - z) % nz, 1) if (i - z) % nz else plane
            pack = jnp.where(lane == i, moved, pack)
        return pack

    def prepare_lines(src, step):
        ex, ey, ez = ([src[c, x] for x in range(nx)] for c in range(3))
        tx_buf[step, 4] = jnp.where(lane == last_z, -COURANT * pltpu.roll(ex[last_x], last_z, 1), 0.0)
        tx_buf[step, 5] = jnp.where(row == last_y, COURANT * pltpu.roll(ex[last_x], last_y, 0), 0.0)
        tx_buf[step, 6] = jnp.where(
            row == last_x, -COURANT * jnp.broadcast_to(src[1, 0, last_y:last_y + 1, :], (ny, nz)), 0.0
        )
        tx_buf[step, 7] = jnp.where(
            lane == last_z, COURANT * pltpu.roll(rows_of(src, None, 1, last_y), last_z, 1), 0.0
        )
        tx_buf[step, 8] = jnp.where(row == last_y, -COURANT * pltpu.roll(lanes_of(ez, last_z), last_y, 0), 0.0)
        at = 2 * nx - 1
        tx_buf[step, 9] = jnp.where(lane == at, COURANT * pltpu.roll(ez[0], (at - last_z) % nz, 1), 0.0)
        tx_buf[step, 0] = rows_of(src, 0, 2, 0)
        tx_buf[step, 1] = lanes_of(ey + ex, 0)

    def prepare_curl(src, step):
        ex, ey, ez = ([src[c, x] for x in range(nx)] for c in range(3))
        for x in range(nx):
            ez_x = ez[x + 1] if x < last_x else zero
            ey_x = ey[x + 1] if x < last_x else zero
            hp[step, 0, x] = src[3, x] - COURANT * ((up_y(ez[x]) - ez[x]) - (up_z(ey[x]) - ey[x]))
            hp[step, 1, x] = src[4, x] - COURANT * ((up_z(ex[x]) - ex[x]) - (ez_x - ez[x]))
            hp[step, 2, x] = src[5, x] - COURANT * ((ey_x - ey[x]) - (up_y(ex[x]) - ex[x]))
        tx_buf[step, 2] = rows_of(hp.at[step], 2, 0, last_y)
        tx_buf[step, 3] = lanes_of([hp[step, 0, x] for x in range(nx)] + [hp[step, 1, x] for x in range(nx)], last_z)

    def halo_copy(src, step, i):
        if i == 0:
            source, target = src.at[pl.ds(1, 2), 0], xlow.at[step]
        elif i == 3:
            source, target = hp.at[step, pl.ds(1, 2), last_x], xhigh.at[step]
        else:
            slot = i - 1 if i < 3 else i - 2
            source, target = tx_buf.at[step, slot], rx_buf.at[step, slot]
        return pltpu.make_async_remote_copy(
            src_ref=source, dst_ref=target, send_sem=send_sem.at[step, i], recv_sem=recv_sem.at[step, i],
            device_id=around(TARGETS[i]), device_id_type=MESH,
        )

    def send(src, step, which):
        for i in which:
            @pl.when(exists(TARGETS[i]))
            def _():
                halo_copy(src, step, i).start()

    def receive(src, step):
        for i in range(12):
            source = exists(tuple(-d for d in TARGETS[i]))

            @pl.when(source)
            def _():
                halo_copy(src, step, i).wait_recv()

            @pl.when(jnp.logical_not(source))
            def _():
                if i == 0:
                    xlow[step] = jnp.zeros(xlow.shape[1:], jnp.float32)
                elif i == 3:
                    xhigh[step] = jnp.zeros(xhigh.shape[1:], jnp.float32)
                else:
                    rx_buf[step, i - 1 if i < 3 else i - 2] = zero

    def sent(src, step):
        for i in range(12):
            @pl.when(exists(TARGETS[i]))
            def _():
                halo_copy(src, step, i).wait_send()

    def advance(src, dst, step, keep, drive, inject):
        y_high = lambda r: jnp.broadcast_to(rx_buf[step, 0, r:r + 1, :], (ny, nz))
        z_pack = rx_buf[step, 1]
        hx, hy, hz = [], [], []
        half = jnp.float32(COURANT)
        for x in range(nx):
            z_of = lambda l: jnp.where(lane == last_z, half * pltpu.roll(z_pack, last_z - l, 1), 0.0)
            y_of = lambda r: jnp.where(row == last_y, half * y_high(r), 0.0)
            hx.append(hp[step, 0, x] + z_of(x) - y_of(nx + x))
            hy.append(hp[step, 1, x] - z_of(nx + x))
            hz.append(hp[step, 2, x] + y_of(x))
        hy[last_x] = hy[last_x] + half * xlow[step, 1]
        hz[last_x] = hz[last_x] - half * xlow[step, 0]
        for x in range(nx):
            dst[3, x], dst[4, x], dst[5, x] = hx[x], hy[x], hz[x]
        hy_x = xhigh[step, 0] + low_exists[0] * src[2, 0] + rx_buf[step, 4]
        hz_x = xhigh[step, 1] - low_exists[0] * src[1, 0] + rx_buf[step, 5]
        y_sign = jnp.where(row < nx, low_exists[1], -low_exists[1])
        z_sign = jnp.where(lane < nx, low_exists[2], -low_exists[2])
        h_y = rx_buf[step, 2] + y_sign * tx_buf[step, 0] + rx_buf[step, 6] + rx_buf[step, 7]
        h_z = rx_buf[step, 3] + z_sign * tx_buf[step, 1] + rx_buf[step, 8] + rx_buf[step, 9]

        def back_y(h, r):
            return h - jnp.where(row == 0, jnp.broadcast_to(h_y[r:r + 1, :], (ny, nz)), pltpu.roll(h, 1, 0))

        def back_z(h, l):
            below = pltpu.roll(h_z, (nz - l) % nz, 1) if l else h_z
            return h - jnp.where(lane == 0, below, pltpu.roll(h, 1, 1))

        for x in range(nx):
            dst[0, x] = keep[x] * src[0, x] + drive[x] * (
                back_y(hz[x], x) - back_z(hy[x], nx + x) + inject[x]
            )
            back_x = hz[x] - (hz[x - 1] if x else hz_x)
            dst[1, x] = keep[x] * src[1, x] + drive[x] * (back_z(hx[x], x) - back_x)
            back_x = hy[x] - (hy[x - 1] if x else hy_x)
            dst[2, x] = keep[x] * src[2, x] + drive[x] * (back_x - back_y(hx[x], nx + x))

    def panel_of(src, step, sigma):
        sums = [zero] * vectors
        for x in range(nx):
            p = sigma[x] * (
                fwd[step, 0, x].astype(jnp.float32) * src[0, x]
                + fwd[step, 1, x].astype(jnp.float32) * src[1, x]
                + fwd[step, 2, x].astype(jnp.float32) * src[2, x]
            )
            pan[step, x] = p
            sums = [s + p * mv[x, n] for n, s in enumerate(sums)]
        message = jnp.zeros((1, nz), jnp.float32)
        one_row = lax.broadcasted_iota(jnp.int32, (1, nz), 1)
        for n in range(vectors):
            total = jnp.sum(jnp.sum(sums[n], axis=0, keepdims=True), axis=1, keepdims=True)
            message = jnp.where(one_row == step * vectors + n, total, message)
        return message

    loads[0].wait()
    prepare_lines(f0, 0)
    prepare_curl(f0, 0)
    pl.semaphore_wait(barrier, expected)
    send(f0, 0, E_FIRST + H_NEXT)

    for load in loads[1:]:
        load.wait()
    sigma, keep, drive = [], [], []
    for x in range(nx):
        found = jnp.zeros((ny, nz), jnp.int32)
        units = rk[x]
        for u in range(unit.shape[0]):
            found = jnp.where(units == u, un[u], found)
        s = found.astype(jnp.float32) * 0.001
        damping = LOSS_FACTOR * s
        sigma.append(s)
        keep.append((1.0 - damping) / (1.0 + damping))
        drive.append(COURANT / (1.0 + damping))

    count = cl.shape[1]
    at = lax.broadcasted_iota(jnp.int32, (nx * ny, count), 0)
    line = (me[0] * nx + at // ny) * (sizes[1] * ny) + me[1] * ny + at % ny
    start = line * (sizes[2] * nz) + me[2] * nz
    where_cells = cl[...]
    in_row = (where_cells >= start) & (where_cells < start + nz)
    spikes = jnp.concatenate([jnp.where(in_row, rs[t], 0.0) for t in range(steps)], axis=0)
    place = lax.broadcasted_iota(jnp.int32, (nz, count), 0)
    hits = jnp.where(place == lax.rem(where_cells, nz), 1.0, 0.0)
    injected = lax.dot_general(
        spikes, hits, (((1,), (1,)), ((), ())), precision=lax.Precision.HIGHEST,
        preferred_element_type=jnp.float32,
    )
    inject = [
        [injected[(t * nx + x) * ny:(t * nx + x + 1) * ny] for x in range(nx)] for t in range(steps)
    ]
    message = panel_of(f0, 0, sigma)

    source = f0
    for step in range(steps):
        target = fin if step == steps - 1 else st.at[step]
        if step > 0:
            prepare_lines(source, step)
            send(source, step, E_FIRST)
            message = message + panel_of(source, step, sigma)
            if step == steps - 1:
                msgs[0][...] = message
                for i, offset in enumerate(stage_offsets(stages[0], sizes)):
                    sum_copy(msgs[0], gathers[0], sum_send[0], sum_recv[0], i, wrapped(offset)).start()
            prepare_curl(source, step)
            send(source, step, H_NEXT)
        receive(source, step)
        advance(source, target, step, keep, drive, inject[step])
        source = target

    for s, stage in enumerate(stages):
        offsets = stage_offsets(stage, sizes)
        if s > 0:
            msgs[s][...] = message
            for i, offset in enumerate(offsets):
                sum_copy(msgs[s], gathers[s], sum_send[s], sum_recv[s], i, wrapped(offset)).start()
        for i, offset in enumerate(offsets):
            sum_copy(msgs[s], gathers[s], sum_send[s], sum_recv[s], i, wrapped(offset)).wait_recv()
        for i in range(len(offsets)):
            message = message + gathers[s][i]
    weights[...] = message

    for step in range(steps):
        sent(f0 if step == 0 else st.at[step - 1], step)
    for s, stage in enumerate(stages):
        for i, offset in enumerate(stage_offsets(stage, sizes)):
            sum_copy(msgs[s], gathers[s], sum_send[s], sum_recv[s], i, wrapped(offset)).wait_send()


def finish(scale, state, pan, weights, state_out, normal_out, nrm, out_sem):
    out_state = pltpu.make_async_copy(state, state_out, out_sem.at[0])
    out_state.start()
    steps, nx, ny, nz = pan.shape
    vectors = nrm.shape[1]
    message = weights[...] * scale
    spread = [jnp.broadcast_to(message[:, i:i + 1], (ny, nz)) for i in range(steps * vectors)]
    for x in range(nx):
        for n in range(vectors):
            total = pan[0, x] * spread[n]
            for k in range(1, steps):
                total = total + pan[k, x] * spread[k * vectors + n]
            nrm[x, n] = total
    out_normal = pltpu.make_async_copy(nrm, normal_out, out_sem.at[1])
    out_normal.start()
    out_state.wait()
    out_normal.wait()


def sum_copy(source, target, send, recv, i, device):
    return pltpu.make_async_remote_copy(
        src_ref=source, dst_ref=target.at[i], send_sem=send.at[i], recv_sem=recv.at[i],
        device_id=device, device_id_type=MESH,
    )


def local(sizes, adjoint_fields, forward_fields, rock_unit, unit_conductivity, receiver_cells, residuals, model_vectors):
    steps = forward_fields.shape[0]
    nx, ny, nz = rock_unit.shape
    units = unit_conductivity.shape[0]
    receivers = receiver_cells.shape[0]
    vectors = model_vectors.shape[1]
    assert adjoint_fields.shape[1] == 1 and 2 * nx <= ny and steps * vectors <= nz
    cell_total = nx * ny * nz * math.prod(sizes)
    scale = 1.0 / math.sqrt(float(steps) * float(cell_total))
    fields = adjoint_fields.reshape(6, nx, ny, nz)
    forward = forward_fields.reshape(steps, 3, nx, ny, nz)
    cells = receiver_cells.reshape(1, receivers)
    stages = reduce_stages(sizes)
    counts = [len(stage_offsets(stage, sizes)) for stage in stages]
    f32 = jnp.float32
    scratch = [
        pltpu.VMEM((6, nx, ny, nz), f32),
        pltpu.VMEM(forward.shape, forward.dtype),
        pltpu.VMEM((nx, ny, nz), jnp.int32),
        pltpu.SMEM((units,), jnp.int32),
        pltpu.VMEM((1, receivers), jnp.int32),
        pltpu.VMEM(residuals.shape, f32),
        pltpu.VMEM(model_vectors.shape, f32),
        pltpu.VMEM((max(steps - 1, 1), 6, nx, ny, nz), f32),
        pltpu.VMEM((steps, 3, nx, ny, nz), f32),
        pltpu.VMEM((steps, 2, ny, nz), f32),
        pltpu.VMEM((steps, 2, ny, nz), f32),
        pltpu.VMEM((steps, 10, ny, nz), f32),
        pltpu.VMEM((steps, 10, ny, nz), f32),
        *[pltpu.VMEM((1, nz), f32) for _ in stages],
        *[pltpu.VMEM((count, 1, nz), f32) for count in counts],
        pltpu.SemaphoreType.DMA((7,)),
        pltpu.SemaphoreType.DMA((steps, 12)),
        pltpu.SemaphoreType.DMA((steps, 12)),
        *[pltpu.SemaphoreType.DMA((count,)) for count in counts],
        *[pltpu.SemaphoreType.DMA((count,)) for count in counts],
    ]
    hbm = pl.BlockSpec(memory_space=pltpu.HBM)
    vmem = pl.BlockSpec(memory_space=pltpu.VMEM)
    state, panel, weights = pl.pallas_call(
        functools.partial(kernel, sizes),
        out_shape=(
            pltpu.VMEM(fields.shape, f32),
            pltpu.VMEM((steps, nx, ny, nz), f32),
            pltpu.VMEM((1, nz), f32),
        ),
        in_specs=[hbm] * 7,
        out_specs=(vmem, vmem, vmem),
        scratch_shapes=scratch,
        compiler_params=pltpu.CompilerParams(
            collective_id=0, has_side_effects=True, vmem_limit_bytes=60 * 2**20
        ),
    )(fields, forward, rock_unit, unit_conductivity, cells, residuals, model_vectors)
    state, normal = pl.pallas_call(
        functools.partial(finish, scale),
        out_shape=(
            jax.ShapeDtypeStruct(fields.shape, f32),
            jax.ShapeDtypeStruct(model_vectors.shape, f32),
        ),
        in_specs=[vmem, vmem, vmem],
        out_specs=(hbm, hbm),
        scratch_shapes=[pltpu.VMEM(model_vectors.shape, f32), pltpu.SemaphoreType.DMA((2,))],
        compiler_params=pltpu.CompilerParams(vmem_limit_bytes=16 * 2**20),
    )(state, panel, weights)
    return state.reshape(adjoint_fields.shape), normal


def solution(mesh):
    sizes = tuple(mesh.shape[a] for a in AXES)
    in_specs = (
        P(None, None, "gx", "gy", "gz"),
        P(None, None, None, "gx", "gy", "gz"),
        P("gx", "gy", "gz"),
        P(),
        P(),
        P(),
        P("gx", None, "gy", "gz"),
    )
    out_specs = (P(None, None, "gx", "gy", "gz"), P("gx", None, "gy", "gz"))
    return jax.shard_map(
        functools.partial(local, sizes), mesh=mesh, in_specs=in_specs, out_specs=out_specs, check_vma=False
    )
```
